128 devices in a mesh: tok: 2 (over y_hi), fin: 16 (over z, x), fout: 4 (over y_lo, core).
Axes of the slice: x: 4, y: 4 (y_hi: 2, y_lo: 2; y = y_hi * 2 + y_lo), z: 4, core: 2. Of those that a mesh axis runs over, the one named last changes fastest.
Arguments:
- tokens: bfloat16 [1024, 6144], P(('tok', 'fout'), 'fin'), may hold values from -6 to 6
- out_grad: bfloat16 [1024, 6144], P(('tok', 'fout'), 'fin'), may hold values from -3 to 3
- up_weight: bfloat16 [6144, 24576], P(('fin', 'tok'), 'fout'), may hold values from -0.078125 to 0.078125
- down_weight: bfloat16 [6144, 24576], P(('fin', 'tok'), 'fout'), may hold values from -0.0390625 to 0.0390625
Outputs:
- grad_tokens: bfloat16 [1024, 6144], P(('tok', 'fout'), 'fin')
- grad_up: float32 [6144, 24576], P(('fin', 'tok'), 'fout')
- grad_down: float32 [6144, 24576], P(('fin', 'tok'), 'fout')
The draws below stay inside these ranges and needn't reach their ends.
All inputs are finite; a program needn't handle non-finite values.
Results may differ from the reference program's by a relative error of at most 0.025.
Values may be sent and summed in bfloat16 or wider, within the bound.
No kernel may reach another device: no remote copies, remote signals or barrier semaphores. Data moves between devices by JAX's collectives and lax.ppermute only.
A program may use at most 128 MiB of HBM per device.

```python
import jax
import jax.numpy as jnp
from jax import lax

D = 6144
FF = 24576
TOKENS = 1024
N_FIN = 16


def shard_levels(own_key, extent, shards, low, largest):
    def one(dim, shards_of):
        steps = jax.random.uniform(jax.random.fold_in(jax.random.fold_in(own_key, 6), dim), (shards_of,), jnp.float32, low / len(shards), largest / len(shards))
        return jnp.repeat(jnp.exp(steps), extent[dim] // shards_of).reshape((-1,) + (1,) * (len(extent) - dim - 1))

    loudness = one(*shards[0])
    for cut in shards[1:]:
        loudness = loudness * one(*cut)
    return loudness


def centred(key, shape, scale, most, shards=(), held_as=jnp.bfloat16):
    array = scale * jax.random.normal(key, shape, jnp.float32)
    if shards:
        array = array * shard_levels(key, shape, shards, -0.22, 0.18)
    return jnp.clip(array, -most, most).astype(held_as)


def setup_inputs(seed: int = 0) -> dict:
    key_list = jax.random.split(jax.random.key(seed), 5)
    tokens = centred(key_list[0], (TOKENS, D), 1.0, 6.0, ((0, 8), (1, 16)))
    out_grad = centred(key_list[1], (TOKENS, D), 0.5, 3.0, ((0, 8), (1, 16)))
    up_weight = centred(key_list[2], (D, FF), D ** -0.5, 0.078125, ((0, 32), (1, 4)))
    down_weight = centred(key_list[3], (D, FF), FF ** -0.5, 0.0390625, ((0, 32), (1, 4)))
    return {"tokens": tokens, "out_grad": out_grad, "up_weight": up_weight, "down_weight": down_weight}


def activate(preact, grad_act):
    activation, pullback = jax.vjp(lambda value: jax.nn.gelu(value, approximate=True), preact)
    grad_pre = pullback(grad_act)[0]
    return (activation.astype(jnp.bfloat16), grad_pre.astype(jnp.bfloat16))

def block_sum(left, weight):
    width = D // N_FIN

    def add_block(total, index):
        start = (index * width).astype(jnp.int32)
        columns = lax.dynamic_slice_in_dim(left, start, width, 1)
        rows = lax.dynamic_slice_in_dim(weight, start, width, 0)
        term = jnp.dot(columns, rows, preferred_element_type=jnp.float32).astype(jnp.bfloat16)
        term = lax.optimization_barrier(term)
        return (total + term.astype(jnp.float32), None)
    start_total = jnp.zeros((left.shape[0], weight.shape[1]), jnp.float32)
    total, _ = lax.scan(add_block, start_total, jnp.arange(N_FIN, dtype=jnp.int32))
    return total

def reference(tokens, out_grad, up_weight, down_weight):
    preact = block_sum(tokens, up_weight)
    grad_act = block_sum(out_grad, down_weight)
    activation, grad_pre = activate(preact, grad_act)
    contract_last = (((1,), (1,)), ((), ()))
    contract_first = (((0,), (0,)), ((), ()))
    grad_tokens = lax.dot_general(grad_pre, up_weight, contract_last, preferred_element_type=jnp.float32).astype(jnp.bfloat16)
    grad_up = lax.dot_general(tokens, grad_pre, contract_first, preferred_element_type=jnp.float32)
    grad_down = lax.dot_general(out_grad, activation, contract_first, preferred_element_type=jnp.float32)
    return (grad_tokens, grad_up, grad_down)
```

```python
import jax
import jax.numpy as jnp
from jax import lax
from jax.sharding import Mesh
from jax.sharding import PartitionSpec as P

AXES = ("yh", "z", "x", "yl", "c")
CHUNKS = ("x", "z")
SWAP = [(0, 1), (1, 0)]


def shift(value, axis, step):
    return lax.ppermute(value, axis, [(i, (i + step) % 4) for i in range(4)])


def swap(value, axis):
    return lax.ppermute(value, axis, SWAP)


def ordered(first, mine, other, axis):
    return jnp.where(
        first, jnp.concatenate([mine, other], axis), jnp.concatenate([other, mine], axis)
    )


def pick(value, index):
    return lax.dynamic_index_in_dim(value, index, 0, keepdims=False)


def activate(preact, grad_act):
    activation, pullback = jax.vjp(lambda value: jax.nn.gelu(value, approximate=True), preact)
    grad_pre = pullback(grad_act)[0]
    return (activation.astype(jnp.bfloat16), grad_pre.astype(jnp.bfloat16))


def gather_tokens(tokens, out_grad, tok, yl, core):
    turned = jnp.stack([tokens.T, out_grad.T])
    rows = turned.shape[1] // 2
    mine = lax.dynamic_slice_in_dim(turned, tok * rows, rows, 1)
    other = lax.dynamic_slice_in_dim(turned, (1 - tok) * rows, rows, 1)
    pair = ordered(tok == 0, mine, swap(other, "yh"), 2)
    quad = ordered(yl == 0, pair, swap(pair, "yl"), 2)
    parts = [quad]
    for axis in ("x", "z"):
        parts += [shift(quad, axis, k) for k in (1, 2, 3)]
    held = jnp.concatenate(parts, 1)
    full = ordered(core == 0, held, swap(held, "c"), 2)
    both = {"x": full[:, : 4 * rows], "z": jnp.concatenate([full[:, :rows], full[:, 4 * rows :]], 1)}
    return both


def spread(up, down, start, width, axis, place):
    got = []
    for k in range(4):
        at = start + lax.rem(place + k, 4) * width
        piece = jnp.concatenate(
            [lax.dynamic_slice_in_dim(w, at, width, 1) for w in (up, down)], 0
        )
        got.append(piece if k == 0 else shift(piece, axis, k))
    rows = up.shape[0]
    return (
        jnp.concatenate([g[:rows] for g in got], 0),
        jnp.concatenate([g[rows:] for g in got], 0),
    )


def scatter_sum(pre, act, axis, place, tok):
    pre = pre.reshape(4, pre.shape[0] // 4, -1)
    act = act.reshape(pre.shape)
    after, across, before = (lax.rem(place + k, 4) for k in (1, 2, 3))
    pre_in = shift(pick(pre, across), axis, 1)
    act_in = shift(pick(act, across), axis, -1)
    f32 = jnp.float32
    bf16 = jnp.bfloat16
    to_after = jnp.stack([(pick(pre, after).astype(f32) + pre_in.astype(f32)).astype(bf16), pick(act, after)])
    to_before = jnp.stack([pick(pre, before), (pick(act, before).astype(f32) + act_in.astype(f32)).astype(bf16)])
    from_before = shift(to_after, axis, 1)
    from_after = shift(to_before, axis, -1)
    own = jnp.stack([pick(pre, place), pick(act, place)])
    total = own.astype(f32) + from_before.astype(f32) + from_after.astype(f32)
    half = total.shape[1] // 2
    mine = lax.dynamic_slice_in_dim(total, tok * half, half, 1)
    other = lax.dynamic_slice_in_dim(total, (1 - tok) * half, half, 1)
    return mine + swap(other.astype(bf16), "yh").astype(f32)


def gather_rows(activation, grad_pre, axis, place, tok):
    mine = jnp.stack([activation, grad_pre])
    pair = ordered(tok == 0, mine, swap(mine, "yh"), 1)
    from_before = shift(pair, axis, 1)
    from_after = shift(pair, axis, -1)
    activ_across = shift(from_before[0], axis, 1)
    grad_across = shift(from_after[1], axis, -1)
    after, across, before = (lax.rem(place + k, 4) for k in (1, 2, 3))
    outs = []
    for own, prev, later, far in (
        (pair[0], from_before[0], from_after[0], activ_across),
        (pair[1], from_before[1], from_after[1], grad_across),
    ):
        full = jnp.zeros((4,) + own.shape, own.dtype)
        for at, block in ((place, own), (before, prev), (after, later), (across, far)):
            full = lax.dynamic_update_slice(full, block[None], (at, 0, 0))
        outs.append(full.reshape(-1, own.shape[1]))
    return outs


def local(tokens, out_grad, up, down):
    f32 = jnp.float32
    bf16 = jnp.bfloat16
    tok, yl, core = lax.axis_index("yh"), lax.axis_index("yl"), lax.axis_index("c")
    place = {"x": lax.axis_index("x"), "z": lax.axis_index("z")}
    rows = up.shape[0]
    width = up.shape[1] // (4 * len(CHUNKS))
    over = {"x": "z", "z": "x"}
    first = (((0,), (0,)), ((), ()))
    last = (((1,), (1,)), ((), ()))
    plain = (((1,), (0,)), ((), ()))

    def mul(a, b, dims):
        return lax.dot_general(a, b, dims, preferred_element_type=f32).astype(bf16)

    weights = [
        spread(up, down, j * 4 * width, width, axis, place[axis]) for j, axis in enumerate(CHUNKS)
    ]
    columns = gather_tokens(tokens, out_grad, tok, yl, core)
    shares = []
    for j, axis in enumerate(CHUNKS):
        x_cols, g_cols = columns[axis][0], columns[axis][1]
        pre = mul(x_cols, weights[j][0], first)
        act = mul(g_cols, weights[j][1], first)
        sums = scatter_sum(pre, act, over[axis], place[over[axis]], tok)
        shares.append(activate(sums[0], sums[1]))
    grad_up = jnp.zeros(up.shape, f32)
    grad_down = jnp.zeros(up.shape, f32)
    tokens_part = {}
    grads = []
    for j, axis in enumerate(CHUNKS):
        activation, grad_pre = gather_rows(*shares[j], over[axis], place[over[axis]], tok)
        part = lax.dot_general(weights[j][0], grad_pre, last, preferred_element_type=f32)
        tokens_part[axis] = tokens_part[axis] + part if axis in tokens_part else part
        grads.append(
            (
                mul(columns[axis][0], grad_pre, plain),
                mul(columns[axis][1], activation, plain),
            )
        )
    held = jnp.concatenate([tokens_part["x"], tokens_part["z"]], 0).astype(bf16)
    half = held.shape[1] // 2
    mine = lax.dynamic_slice_in_dim(held, core * half, half, 1).astype(f32)
    other = lax.dynamic_slice_in_dim(held, (1 - core) * half, half, 1)
    held = mine + swap(other, "c").astype(f32)
    total = held[:rows] + held[4 * rows : 5 * rows]
    held = held.astype(bf16)
    for base, axis in ((0, "x"), (4, "z")):
        for k in (1, 2, 3):
            piece = held[(base + k) * rows : (base + k + 1) * rows]
            total = total + shift(piece, axis, -k).astype(f32)
    for axis, at in (("yl", yl), ("yh", tok)):
        half = total.shape[1] // 2
        mine = lax.dynamic_slice_in_dim(total, at * half, half, 1)
        other = lax.dynamic_slice_in_dim(total, (1 - at) * half, half, 1).astype(bf16)
        got = swap(other, axis)
        if axis == "yl":
            total = mine + got.astype(f32)
        else:
            grad_tokens = ordered(tok == 0, mine.astype(bf16), got, 0).T

    for j, axis in enumerate(CHUNKS):
        for k in range(4):
            piece = jnp.concatenate([g[k * rows : (k + 1) * rows] for g in grads[j]], 0)
            if k:
                piece = shift(piece, axis, -k)
            at = j * 4 * width + lax.rem(place[axis] + k, 4) * width
            grad_up = lax.dynamic_update_slice(grad_up, piece[:rows].astype(f32), (0, at))
            grad_down = lax.dynamic_update_slice(grad_down, piece[rows:].astype(f32), (0, at))
    return (grad_tokens, grad_up, grad_down)


def solution(mesh):
    cube = Mesh(mesh.devices.reshape(2, 4, 4, 2, 2), AXES)
    rows = P(("yh", "yl", "c"), ("z", "x"))
    weight = P(("z", "x", "yh"), ("yl", "c"))
    return jax.shard_map(
        local,
        mesh=cube,
        in_specs=(rows, rows, weight, weight),
        out_specs=(rows, weight, weight),
        check_vma=False,
    )
```

```python
import jax
import jax.numpy as jnp
from jax import lax
from jax.sharding import Mesh
from jax.sharding import PartitionSpec as P

AXES = ("yh", "z", "x", "yl", "c")
CHUNKS = 2
SWAP = [(0, 1), (1, 0)]


def ring(step, along_x):
    pairs = []
    for z in range(4):
        for x in range(4):
            for c in range(2):
                to = (z, (x + step) % 4) if (c == 0) == along_x else ((z + step) % 4, x)
                pairs.append(((z * 4 + x) * 2 + c, (to[0] * 4 + to[1]) * 2 + c))
    return pairs


def deal(value, step):
    return lax.ppermute(value, ("z", "x", "c"), ring(step, True))


def pass_on(value, step):
    return lax.ppermute(value, ("z", "x", "c"), ring(step, False))


def swap(value, axis):
    return lax.ppermute(value, axis, SWAP)


def ordered(first, mine, other, axis):
    return jnp.where(
        first, jnp.concatenate([mine, other], axis), jnp.concatenate([other, mine], axis)
    )


def pick(value, index):
    return lax.dynamic_index_in_dim(value, index, 0, keepdims=False)


def halves(value, index, axis):
    half = value.shape[axis] // 2
    return (
        lax.dynamic_slice_in_dim(value, index * half, half, axis),
        lax.dynamic_slice_in_dim(value, (1 - index) * half, half, axis),
    )


def activate(preact, grad_act):
    activation, pullback = jax.vjp(lambda value: jax.nn.gelu(value, approximate=True), preact)
    grad_pre = pullback(grad_act)[0]
    return (activation.astype(jnp.bfloat16), grad_pre.astype(jnp.bfloat16))


def gather_tokens(tokens, out_grad, tok, yl, core):
    turned = jnp.stack([tokens.T, out_grad.T])
    held, other = halves(turned, tok, 1)
    held = ordered(tok == 0, held, swap(other, "yh"), 2)
    held = ordered(yl == 0, held, swap(held, "yl"), 2)
    held = ordered(core == 0, held, swap(held, "c"), 2)
    parts = [held] + [deal(held, k) for k in (1, 2, 3)]
    return [jnp.concatenate([p[i] for p in parts], 0) for i in range(2)]


def spread(up, down, start, width, place):
    got = []
    for k in range(4):
        at = start + lax.rem(place + k, 4) * width
        piece = jnp.concatenate(
            [lax.dynamic_slice_in_dim(w, at, width, 1) for w in (up, down)], 0
        )
        got.append(piece if k == 0 else deal(piece, k))
    rows = up.shape[0]
    return (
        jnp.concatenate([g[:rows] for g in got], 0),
        jnp.concatenate([g[rows:] for g in got], 0),
    )


def scatter_sum(pre, act, place, tok):
    f32 = jnp.float32
    bf16 = jnp.bfloat16
    pre = pre.reshape(4, pre.shape[0] // 4, -1)
    act = act.reshape(pre.shape)
    after, across, before = (lax.rem(place + k, 4) for k in (1, 2, 3))
    pre_in = pass_on(pick(pre, across), 1)
    act_in = pass_on(pick(act, across), -1)
    to_after = jnp.stack([(pick(pre, after).astype(f32) + pre_in.astype(f32)).astype(bf16), pick(act, after)])
    to_before = jnp.stack([pick(pre, before), (pick(act, before).astype(f32) + act_in.astype(f32)).astype(bf16)])
    from_before = pass_on(to_after, 1)
    from_after = pass_on(to_before, -1)
    own = jnp.stack([pick(pre, place), pick(act, place)])
    total = own.astype(f32) + from_before.astype(f32) + from_after.astype(f32)
    mine, other = halves(total, tok, 1)
    return mine + swap(other.astype(bf16), "yh").astype(f32)


def gather_rows(activation, grad_pre, place, tok):
    mine = jnp.stack([activation, grad_pre])
    pair = ordered(tok == 0, mine, swap(mine, "yh"), 1)
    from_before = pass_on(pair, 1)
    from_after = pass_on(pair, -1)
    activ_across = pass_on(from_before[0], 1)
    grad_across = pass_on(from_after[1], -1)
    after, across, before = (lax.rem(place + k, 4) for k in (1, 2, 3))
    outs = []
    for own, prev, later, far in (
        (pair[0], from_before[0], from_after[0], activ_across),
        (pair[1], from_before[1], from_after[1], grad_across),
    ):
        full = jnp.zeros((4,) + own.shape, own.dtype)
        for at, block in ((place, own), (before, prev), (after, later), (across, far)):
            full = lax.dynamic_update_slice(full, block[None], (at, 0, 0))
        outs.append(full.reshape(-1, own.shape[1]))
    return outs


def local(tokens, out_grad, up, down):
    f32 = jnp.float32
    bf16 = jnp.bfloat16
    tok, yl, core = lax.axis_index("yh"), lax.axis_index("yl"), lax.axis_index("c")
    x, z = lax.axis_index("x"), lax.axis_index("z")
    dealt = jnp.where(core == 0, x, z)
    summed = jnp.where(core == 0, z, x)
    rows = up.shape[0]
    width = up.shape[1] // (4 * CHUNKS)
    first = (((0,), (0,)), ((), ()))
    last = (((1,), (1,)), ((), ()))
    plain = (((1,), (0,)), ((), ()))

    def mul(a, b, dims):
        return lax.dot_general(a, b, dims, preferred_element_type=f32).astype(bf16)

    weights = [spread(up, down, j * 4 * width, width, dealt) for j in range(CHUNKS)]
    x_cols, g_cols = gather_tokens(tokens, out_grad, tok, yl, core)
    shares = []
    for j in range(CHUNKS):
        pre = mul(x_cols, weights[j][0], first)
        act = mul(g_cols, weights[j][1], first)
        sums = scatter_sum(pre, act, summed, tok)
        shares.append(activate(sums[0], sums[1]))
    part = 0
    grads = []
    for j in range(CHUNKS):
        activation, grad_pre = gather_rows(*shares[j], summed, tok)
        part = part + lax.dot_general(weights[j][0], grad_pre, last, preferred_element_type=f32)
        grads.append((mul(x_cols, grad_pre, plain), mul(g_cols, activation, plain)))
    held = part.astype(bf16)
    total = part[:rows]
    for k in (1, 2, 3):
        total = total + deal(held[k * rows : (k + 1) * rows], -k).astype(f32)
    for axis, at in (("c", core), ("yl", yl)):
        mine, other = halves(total, at, 1)
        total = mine + swap(other.astype(bf16), axis).astype(f32)
    mine, other = halves(total.astype(bf16), tok, 1)
    grad_tokens = ordered(tok == 0, mine, swap(other, "yh"), 0).T

    grad_up = jnp.zeros(up.shape, f32)
    grad_down = jnp.zeros(up.shape, f32)
    for j in range(CHUNKS):
        for k in range(4):
            piece = jnp.concatenate([g[k * rows : (k + 1) * rows] for g in grads[j]], 0)
            if k:
                piece = deal(piece, -k)
            at = j * 4 * width + lax.rem(dealt + k, 4) * width
            grad_up = lax.dynamic_update_slice(grad_up, piece[:rows].astype(f32), (0, at))
            grad_down = lax.dynamic_update_slice(grad_down, piece[rows:].astype(f32), (0, at))
    return (grad_tokens, grad_up, grad_down)


def solution(mesh):
    cube = Mesh(mesh.devices.reshape(2, 4, 4, 2, 2), AXES)
    rows = P(("yh", "yl", "c"), ("z", "x"))
    weight = P(("z", "x", "yh"), ("yl", "c"))
    return jax.shard_map(
        local,
        mesh=cube,
        in_specs=(rows, rows, weight, weight),
        out_specs=(rows, weight, weight),
        check_vma=False,
    )
```

```python
import jax
import jax.numpy as jnp
from jax import lax
from jax.experimental import pallas as pl
from jax.sharding import Mesh
from jax.sharding import PartitionSpec as P

AXES = ("yh", "z", "x", "yl", "c")
CHUNKS = 2
SWAP = [(0, 1), (1, 0)]
F32 = jnp.float32
BF16 = jnp.bfloat16


def ring(step, along_x):
    pairs = []
    for z in range(4):
        for x in range(4):
            for c in range(2):
                to = (z, (x + step) % 4) if (c == 0) == along_x else ((z + step) % 4, x)
                pairs.append(((z * 4 + x) * 2 + c, (to[0] * 4 + to[1]) * 2 + c))
    return pairs


def deal(value, step):
    return lax.ppermute(value, ("z", "x", "c"), ring(step, True))


def pass_on(value, step):
    return lax.ppermute(value, ("z", "x", "c"), ring(step, False))


def swap(value, axis):
    return lax.ppermute(value, axis, SWAP)


def after(values, *others):
    return lax.optimization_barrier((tuple(values), others))[0]


def ordered(first, mine, other, axis):
    return jnp.where(
        first, jnp.concatenate([mine, other], axis), jnp.concatenate([other, mine], axis)
    )


def halves(value, index, axis):
    half = value.shape[axis] // 2
    return (
        lax.dynamic_slice_in_dim(value, index * half, half, axis),
        lax.dynamic_slice_in_dim(value, (1 - index) * half, half, axis),
    )


def rotated(value, by):
    width = value.shape[-1]
    return lax.dynamic_slice_in_dim(
        jnp.concatenate([value, value], -1), by * (width // 4), width, value.ndim - 1
    )


def mul(a, b, left, right):
    return lax.dot_general(a, b, (((left,), (right,)), ((), ())), preferred_element_type=F32)


def activate(preact, grad_act):
    activation, pullback = jax.vjp(lambda value: jax.nn.gelu(value, approximate=True), preact)
    grad_pre = pullback(grad_act)[0]
    return jnp.stack([grad_pre.astype(BF16), activation.astype(BF16)])


def weight_piece(up, down, at, width):
    return jnp.concatenate([lax.dynamic_slice_in_dim(w, at, width, 1) for w in (up, down)], 0)


def unwritten(shape):
    return pl.pallas_call(
        lambda out: None,
        out_shape=jax.ShapeDtypeStruct(shape, F32),
        out_specs=pl.BlockSpec(memory_space=pl.ANY),
    )()


def local(tokens, out_grad, up, down):
    tok, yl, core = lax.axis_index("yh"), lax.axis_index("yl"), lax.axis_index("c")
    x, z = lax.axis_index("x"), lax.axis_index("z")
    dealt = jnp.where(core == 0, x, z)
    summed = jnp.where(core == 0, z, x)
    rows = up.shape[0]
    whole = up.shape[1] // 4
    width = whole // CHUNKS
    order = (1, 3, 2)
    starts = {k: lax.rem(dealt + k, 4) * whole for k in range(4)}

    turned = jnp.stack([tokens.T, out_grad.T])
    held, other = halves(turned, tok, 1)
    got = [deal(weight_piece(up, down, starts[k], whole), k) for k in order]
    held = ordered(tok == 0, held, swap(other, "yh"), 2)
    held = ordered(yl == 0, held, swap(held, "yl"), 2)
    held = ordered(core == 0, held, swap(held, "c"), 2)
    held = rotated(held, summed)
    (held,) = after((held,), *got)
    parts = [held] + [deal(held, k) for k in order]
    got = [weight_piece(*after((up, down), held), starts[0], whole)] + got
    weights = [jnp.concatenate([w[i * rows : (i + 1) * rows] for w in got], 0) for i in range(2)]
    weights = [[w[:, j * width : (j + 1) * width] for w in weights] for j in range(CHUNKS)]
    columns = [jnp.concatenate([p[i] for p in parts], 0) for i in range(2)]

    shares = []
    for j in range(CHUNKS):
        pre, act = (
            mul(columns[i], weights[j][i], 0, 0).astype(BF16).reshape(4, -1, width) for i in range(2)
        )
        pre_in, act_in = pass_on(pre[2], 1), pass_on(act[2], -1)
        later = jnp.stack([(pre[1].astype(F32) + pre_in.astype(F32)).astype(BF16), act[1]])
        before = jnp.stack([pre[3], (act[3].astype(F32) + act_in.astype(F32)).astype(BF16)])
        total = jnp.stack([pre[0], act[0]]).astype(F32)
        total = total + pass_on(later, 1).astype(F32) + pass_on(before, -1).astype(F32)
        total = total + swap(total.astype(BF16), "yh").astype(F32)
        shares.append(activate(total[0], total[1]))

    grads = []
    part = 0.0
    for j in range(CHUNKS):
        mine = shares[j]
        from_before, from_after = pass_on(mine, 1), pass_on(mine, -1)
        far = (pass_on(from_before[0], 1), pass_on(from_after[1], -1))
        full = [
            jnp.concatenate([mine[i], from_after[i], far[i], from_before[i]], 0) for i in range(2)
        ]
        grads.append([mul(columns[i], full[i], 1, 0).astype(BF16) for i in range(2)])
        part += mul(weights[j][0], full[0], 1, 1)
    part = part.astype(BF16)

    total = part[:rows].astype(F32)
    for i, k in enumerate(order, 1):
        total = total + deal(part[i * rows : (i + 1) * rows], -k).astype(F32)
    total = rotated(total, lax.rem(4 - summed, 4))
    for axis, at in (("c", core), ("yl", yl)):
        mine, other = halves(total, at, 1)
        total = mine + swap(other.astype(BF16), axis).astype(F32)
    mine, other = halves(total.astype(BF16), tok, 1)
    grad_tokens = ordered(tok == 0, mine, swap(other, "yh"), 0).T

    outs = [unwritten(up.shape) for _ in range(2)]
    for j in range(CHUNKS):
        for i, k in enumerate((0,) + order):
            piece = jnp.concatenate([g[i * rows : (i + 1) * rows] for g in grads[j]], 0)
            if i:
                piece = deal(piece, -k)
            at = (0, starts[k] + j * width)
            outs = [
                lax.dynamic_update_slice(o, p.astype(F32), at)
                for o, p in zip(outs, (piece[:rows], piece[rows:]))
            ]
    return (grad_tokens, *outs)


def solution(mesh):
    cube = Mesh(mesh.devices.reshape(2, 4, 4, 2, 2), AXES)
    rows = P(("yh", "yl", "c"), ("z", "x"))
    weight = P(("z", "x", "yh"), ("yl", "c"))
    return jax.shard_map(
        local,
        mesh=cube,
        in_specs=(rows, rows, weight, weight),
        out_specs=(rows, weight, weight),
        check_vma=False,
    )
```

```python
import jax
import jax.numpy as jnp
from jax import lax
from jax.experimental import pallas as pl
from jax.sharding import Mesh
from jax.sharding import PartitionSpec as P

AXES = ("yh", "z", "x", "yl", "c")
CHUNKS = 2
SWAP = [(0, 1), (1, 0)]
F32 = jnp.float32
BF16 = jnp.bfloat16


def ring(step, along_x):
    pairs = []
    for z in range(4):
        for x in range(4):
            for c in range(2):
                to = (z, (x + step) % 4) if (c == 0) == along_x else ((z + step) % 4, x)
                pairs.append(((z * 4 + x) * 2 + c, (to[0] * 4 + to[1]) * 2 + c))
    return pairs


def deal(value, step):
    return lax.ppermute(value, ("z", "x", "c"), ring(step, True))


def pass_on(value, step):
    return lax.ppermute(value, ("z", "x", "c"), ring(step, False))


def swap(value, axis):
    return lax.ppermute(value, axis, SWAP)


def after(values, *others):
    return lax.optimization_barrier((tuple(values), others))[0]


def ordered(first, mine, other, axis):
    return jnp.where(
        first, jnp.concatenate([mine, other], axis), jnp.concatenate([other, mine], axis)
    )


def halves(value, index, axis):
    half = value.shape[axis] // 2
    return (
        lax.dynamic_slice_in_dim(value, index * half, half, axis),
        lax.dynamic_slice_in_dim(value, (1 - index) * half, half, axis),
    )


def rotated(value, by):
    width = value.shape[-1]
    return lax.dynamic_slice_in_dim(
        jnp.concatenate([value, value], -1), by * (width // 4), width, value.ndim - 1
    )


def mul(a, b, left, right):
    return lax.dot_general(a, b, (((left,), (right,)), ((), ())), preferred_element_type=F32)


def activate(preact, grad_act):
    activation, pullback = jax.vjp(lambda value: jax.nn.gelu(value, approximate=True), preact)
    grad_pre = pullback(grad_act)[0]
    return jnp.stack([grad_pre.astype(BF16), activation.astype(BF16)])


def weight_piece(up, down, at, width):
    return jnp.concatenate([lax.dynamic_slice_in_dim(w, at, width, 1) for w in (up, down)], 0)


def unwritten(shape):
    return pl.pallas_call(
        lambda out: None,
        out_shape=jax.ShapeDtypeStruct(shape, F32),
        out_specs=pl.BlockSpec(memory_space=pl.ANY),
    )()


def local(tokens, out_grad, up, down):
    tok, yl, core = lax.axis_index("yh"), lax.axis_index("yl"), lax.axis_index("c")
    x, z = lax.axis_index("x"), lax.axis_index("z")
    dealt = jnp.where(core == 0, x, z)
    summed = jnp.where(core == 0, z, x)
    rows = up.shape[0]
    whole = up.shape[1] // 4
    width = whole // CHUNKS
    order = (1, 3, 2)
    starts = {k: lax.rem(dealt + k, 4) * whole for k in range(4)}

    turned = jnp.stack([tokens.T, out_grad.T])
    held, other = halves(turned, tok, 1)
    got = [deal(weight_piece(up, down, starts[k], whole), k) for k in order]
    held = ordered(tok == 0, held, swap(other, "yh"), 2)
    held = ordered(yl == 0, held, swap(held, "yl"), 2)
    held = ordered(core == 0, held, swap(held, "c"), 2)
    held = rotated(held, summed)
    (held,) = after((held,), *got)
    parts = [held] + [deal(held, k) for k in order]
    got = [weight_piece(*after((up, down), held), starts[0], whole)] + got
    weights = [jnp.concatenate([w[i * rows : (i + 1) * rows] for w in got], 0) for i in range(2)]
    weights = [[w[:, j * width : (j + 1) * width] for w in weights] for j in range(CHUNKS)]
    columns = [jnp.concatenate([p[i] for p in parts], 0) for i in range(2)]

    shares = []
    for j in range(CHUNKS):
        pre, act = (
            mul(columns[i], weights[j][i], 0, 0).astype(BF16).reshape(4, -1, width) for i in range(2)
        )
        pre_in, act_in = pass_on(pre[2], 1), pass_on(act[2], -1)
        later = jnp.stack([(pre[1].astype(F32) + pre_in.astype(F32)).astype(BF16), act[1]])
        before = jnp.stack([pre[3], (act[3].astype(F32) + act_in.astype(F32)).astype(BF16)])
        total = jnp.stack([pre[0], act[0]]).astype(F32)
        total = total + pass_on(later, 1).astype(F32) + pass_on(before, -1).astype(F32)
        total = total + swap(total.astype(BF16), "yh").astype(F32)
        shares.append(activate(total[0], total[1]))

    grads = []
    part = 0.0
    for j in range(CHUNKS):
        mine = shares[j]
        from_before, from_after = pass_on(mine, 1), pass_on(mine, -1)
        far = (pass_on(from_before[0], 1), pass_on(from_after[1], -1))
        full = [
            jnp.concatenate([mine[i], from_after[i], far[i], from_before[i]], 0) for i in range(2)
        ]
        grads.append([mul(columns[i], full[i], 1, 0).astype(BF16) for i in range(2)])
        part += mul(weights[j][0], full[0], 1, 1)
    part = part.astype(BF16)

    total = part[:rows].astype(F32)
    for i, k in enumerate(order, 1):
        total = total + deal(part[i * rows : (i + 1) * rows], -k).astype(F32)
    total = rotated(total, lax.rem(4 - summed, 4))
    for axis, at in (("c", core), ("yl", yl)):
        mine, other = halves(total, at, 1)
        total = mine + swap(other.astype(BF16), axis).astype(F32)
    mine, other = halves(total.astype(BF16), tok, 1)
    grad_tokens = ordered(tok == 0, mine, swap(other, "yh"), 0).T

    outs = [unwritten(up.shape) for _ in range(2)]
    for i, k in enumerate((0,) + order):
        rows_of = [[g[i * rows : (i + 1) * rows] for g in pair] for pair in grads]
        piece = jnp.concatenate([jnp.concatenate(pair, 0) for pair in rows_of], 1)
        if i:
            piece = deal(piece, -k)
        at = (0, starts[k])
        outs = [
            lax.dynamic_update_slice(o, p.astype(F32), at)
            for o, p in zip(outs, (piece[:rows], piece[rows:]))
        ]
    return (grad_tokens, *outs)


def solution(mesh):
    cube = Mesh(mesh.devices.reshape(2, 4, 4, 2, 2), AXES)
    rows = P(("yh", "yl", "c"), ("z", "x"))
    weight = P(("z", "x", "yh"), ("yl", "c"))
    return jax.shard_map(
        local,
        mesh=cube,
        in_specs=(rows, rows, weight, weight),
        out_specs=(rows, weight, weight),
        check_vma=False,
    )
```
